512 devices in a mesh: section: 32 (over y, x), expert: 16 (over z, core).
Axes of the slice: x: 4, y: 8, z: 8, core: 2. Of those that a mesh axis runs over, the one named last changes fastest.
Arguments:
- acts: bfloat16 [32, 2, 512, 6144], P('section', None, 'expert'), may hold values from -3 to 3
- routed_expert_index: int32 [32, 2, 512, 2], P('section', None, 'expert'), may hold values from 0 to 63, all different within a row; in each aligned block of 32 rows (0 to 31, 32 to 63, ..., all dimensions but the last counted through in order) at most 2 rows name the same one
- routed_expert_scores: float32 [32, 2, 512, 2], P('section', None, 'expert'), may hold values from -0.75 to 0.75
- section_norm_scale: float32 [32, 6144], P('section'), may hold values from 0.1 to 1.9
- adapter_down_weight: bfloat16 [32, 64, 16, 6144], P('section', 'expert'), may hold values from -0.078125 to 0.078125
- adapter_up_weight: bfloat16 [32, 64, 16, 6144], P('section', 'expert'), may hold values from -1.5 to 1.5
Outputs:
- handed: bfloat16 [32, 2, 512, 6144], P('section', None, 'expert')
The draws below stay inside these ranges and needn't reach their ends.
Inputs may be any that keep to these rules, and one draw needn't show every extreme that they name: `routed_expert_index`: within one micro-batch, the 32 tokens of one index of expert name no expert more than 2 times; a token's two experts differ.
All inputs are finite; a program needn't handle non-finite values.
Results may differ from the reference program's by a relative error of at most 0.0095.
Values may be sent and summed in bfloat16 or wider, within the bound.
A program may use at most 64 MiB of HBM per device.

```python
import math
import jax
import jax.numpy as jnp
import numpy as np
from jax import lax

MODEL_WIDTH = 6144
ADAPTER_RANK = 16
TOP = 2
MB = 2
MB_TOK = 32
ADAPTER_EXPERTS = 64
CAP = 2
TOKS = 512
RELAY_SECTIONS = 32


def block_scale(stream_key, dims, split, least, largest):
    gain, own = 1.0, jax.random.fold_in(stream_key, 6)
    for dim, parts in split:
        steps = jnp.exp(jax.random.uniform(jax.random.fold_in(own, dim), (parts,), jnp.float32, least / len(split), largest / len(split)))
        gain = gain * jnp.repeat(steps, dims[dim] // parts).reshape([-1 if axis == dim else 1 for axis in range(len(dims))])
    return gain


def shared_out(rng, own, number, rows, amount, top, bound, lean):
    ranking = jax.random.permutation(rng, amount)
    crowded, usual = portions_of(amount, rows * top, bound, lean, True), portions_of(amount, rows * top, bound, lean, False)
    places = jnp.arange(amount)

    def named(lengths, rotation):
        used = int((lengths > 0).sum())
        fixed = max(1, used // 4)
        passed = fixed + (places - fixed + rotation * (used - fixed)) % max(1, amount - fixed)
        return jnp.zeros((amount,), jnp.int32).at[ranking[jnp.where(places < fixed, places, passed)]].set(jnp.asarray(lengths, jnp.int32))

    lengths = jnp.where(number % 4 == 0, named(crowded, number // 4), named(usual, number - number // 4 - 1))
    mixed = jax.random.permutation(jax.random.fold_in(own, 3), amount)
    donor, receiver = mixed[0:amount // 2 * 2:2], mixed[1:amount // 2 * 2:2]
    slack = jnp.minimum(lengths[donor] - 1, bound - lengths[receiver]) // 2
    slack = jnp.where((donor == ranking[0]) | (receiver == ranking[0]) | (lengths[receiver] == 0), 0, jnp.maximum(slack, 0))
    passed = jax.random.randint(jax.random.fold_in(own, 4), (amount // 2,), 0, 1 << 20) % (slack + 1)
    lengths = lengths.at[donor].add(-passed).at[receiver].add(passed)
    items = jnp.searchsorted(jnp.cumsum(lengths), jnp.arange(rows * top), side="right").astype(jnp.int32)
    grid = items.reshape(top, rows).T
    grid = grid[jax.random.permutation(jax.random.fold_in(own, 1), rows)]
    rotation = jax.random.randint(jax.random.fold_in(own, 2), (rows, 1), 0, top)
    return jnp.take_along_axis(grid, (jnp.arange(top)[None, :] + rotation) % top, axis=1)


def portions_of(count, total, reach, skew, full):
    loads = [(1 << 20) // math.isqrt(grade ** skew) + 1 for grade in range(1, count + 1)]
    largest = reach if full else min(reach, max(-(-total // count), total * loads[0] // sum(loads)))
    least = 1 if total - largest >= count - 1 else 0
    given, surplus = [largest] + [least] * (count - 1), total - largest - least * (count - 1)
    while surplus > 0:
        free = [i for i in range(1, count) if given[i] < largest] or [i for i in range(1, count) if given[i] < reach]
        pool, budget = sum([loads[i] for i in free]), surplus
        for i in free:
            more = min(reach - given[i], max(1, budget * loads[i] // pool), surplus)
            given[i] = given[i] + more
            surplus = surplus - more
    return np.array(given)


def centred(rng, dims, width, bound, pieces=(), kind=jnp.bfloat16):
    drawn = jax.random.normal(rng, dims, jnp.float32) * width
    if len(pieces) > 0:
        drawn = block_scale(rng, dims, pieces, -0.22, 0.18) * drawn
    return jnp.clip(drawn, min=-bound, max=bound).astype(kind)


def setup_inputs(seed: int = 0) -> dict:
    arg_keys = jax.random.split(jax.random.key(seed), 7)
    acts = centred(arg_keys[0], (RELAY_SECTIONS, MB, TOKS, MODEL_WIDTH), 0.5, 3.0, ((0, 32), (2, 16)))
    routed_expert_index_keys = jax.random.split(jax.random.fold_in(arg_keys[1], 1), RELAY_SECTIONS * MB * TOKS // MB_TOK)
    routed_expert_index_turns = jax.random.permutation(jax.random.fold_in(arg_keys[1], 3), RELAY_SECTIONS * MB * TOKS // MB_TOK)
    routed_expert_index = jax.vmap(lambda own, number: shared_out(jax.random.fold_in(arg_keys[1], 2), own, number, MB_TOK, ADAPTER_EXPERTS, TOP, CAP, 1))(routed_expert_index_keys, routed_expert_index_turns).reshape((RELAY_SECTIONS, MB, TOKS, TOP))
    routed_expert_scores = jnp.clip(jax.random.uniform(arg_keys[2], (RELAY_SECTIONS, MB, TOKS, TOP), jnp.float32, -0.75, 0.75) * block_scale(arg_keys[2], (RELAY_SECTIONS, MB, TOKS, TOP), ((0, 32), (2, 16)), -0.4, 0.0), -0.75, 0.75)
    section_norm_scale = jnp.clip(1.0 + 0.18 * jax.random.normal(arg_keys[3], (RELAY_SECTIONS, MODEL_WIDTH), jnp.float32), 0.1, 1.9)
    adapter_down_weight = centred(arg_keys[4], (RELAY_SECTIONS, ADAPTER_EXPERTS, ADAPTER_RANK, MODEL_WIDTH), MODEL_WIDTH ** -0.5, 0.078125, ((0, 32), (1, 16)))
    adapter_up_weight = centred(arg_keys[5], (RELAY_SECTIONS, ADAPTER_EXPERTS, ADAPTER_RANK, MODEL_WIDTH), ADAPTER_RANK ** -0.5, 1.5, ((0, 32), (1, 16)))
    return {"acts": acts, "routed_expert_index": routed_expert_index, "routed_expert_scores": routed_expert_scores, "section_norm_scale": section_norm_scale, "adapter_down_weight": adapter_down_weight, "adapter_up_weight": adapter_up_weight}


def relay_section_layer(token_entry):
    acts, routed_expert_index, routed_expert_scores, section_norm_scale, adapter_down_weight, adapter_up_weight = token_entry
    row_blocks = acts.reshape(-1, MB_TOK, MODEL_WIDTH)
    id_blocks = routed_expert_index.reshape(-1, MB_TOK, TOP)
    logit_blocks = routed_expert_scores.reshape(-1, MB_TOK, TOP)

    def block(block_items):
        acts_block, selected_expert, logits = block_items
        rows_float = acts_block.astype(jnp.float32)
        inverse = lax.rsqrt(lax.optimization_barrier(jnp.mean(rows_float * rows_float, axis=-1, keepdims=True)) + 1e-05)
        normed = (rows_float * inverse * section_norm_scale[None, :]).astype(jnp.bfloat16)
        down_projected_rows = adapter_down_weight[selected_expert].astype(jnp.float32)
        low_rank = jnp.einsum('td,tkrd->tkr', normed.astype(jnp.float32), down_projected_rows).astype(jnp.bfloat16)
        up_projected_rows = adapter_up_weight[selected_expert].astype(jnp.float32)
        deltas = jnp.einsum('tkr,tkrd->tkd', low_rank.astype(jnp.float32), up_projected_rows).astype(jnp.bfloat16)
        first_gate = 1.0 / (1.0 + jnp.exp(logits[:, 1] - logits[:, 0]))
        second_gate = 1.0 / (1.0 + jnp.exp(logits[:, 0] - logits[:, 1]))
        gate_pair = jnp.stack([first_gate, second_gate], axis=1)
        mixed_rows = rows_float + lax.optimization_barrier(jnp.sum(gate_pair[:, :, None] * deltas.astype(jnp.float32), axis=1))
        return mixed_rows.astype(jnp.bfloat16)
    outputs = lax.map(block, (row_blocks, id_blocks, logit_blocks))
    return outputs.reshape(acts.shape)

def reference(acts, routed_expert_index, routed_expert_scores, section_norm_scale, adapter_down_weight, adapter_up_weight):
    layer_output = lax.map(relay_section_layer, (acts, routed_expert_index, routed_expert_scores, section_norm_scale, adapter_down_weight, adapter_up_weight))
    return jnp.roll(layer_output, 1, axis=0)
```

```python
import jax
import jax.numpy as jnp
from jax import lax
from jax.experimental import pallas as pl
from jax.experimental.pallas import tpu as pltpu
from jax.sharding import PartitionSpec as P

MESH = pl.DeviceIdType.MESH
SECTIONS = 32
CHIPS = 8
GROUP = 16
MB = 2
TOK = 32
RANK = 16
LOCAL_EXPERTS = 4
WIDTH = 6144
SLICE = WIDTH // GROUP
BLOCK = 2 * MB * TOK
F32 = jnp.float32
BF16 = jnp.bfloat16


def kernel(
    acts,
    index,
    scores,
    gain,
    down,
    up,
    out,
    own_acts,
    acts_in,
    down_in,
    up_in,
    flat,
    meta,
    part,
    red,
    low,
    mixed,
    send_out,
    hand,
    local_sem,
    acts_ss,
    acts_rs,
    down_ss,
    down_rs,
    up_ss,
    up_rs,
    meta_ss,
    meta_rs,
    part_ss,
    part_rs,
    low_ss,
    low_rs,
    out_ss,
    out_rs,
    hand_ss,
    hand_rs,
):
    s = lax.axis_index("section")
    e = lax.axis_index("expert")
    z = e // 2
    c = lax.rem(e, 2)
    s_next = lax.rem(s + 1, SECTIONS)
    s_prev = lax.rem(s + SECTIONS - 1, SECTIONS)

    def hop(j):
        return 4 + ((j + 1) // 2) * (1 - 2 * lax.rem(j, 2))

    def peer(i):
        return lax.rem(z + hop(i // 2), CHIPS) * 2 + lax.rem(c + 1 - lax.rem(i, 2), 2)

    def source(i):
        return lax.rem(z + CHIPS - hop(i // 2), CHIPS) * 2 + lax.rem(c + 1 - lax.rem(i, 2), 2)

    def lanes(k, width):
        return pl.ds(pl.multiple_of(k * width, width), width)

    def each(count, body):
        def step(i, carry):
            body(i)
            return carry

        lax.fori_loop(0, count, step, 0)

    barrier = pltpu.get_barrier_semaphore()

    def greet(i):
        pl.semaphore_signal(barrier, inc=1, device_id=(s, peer(i)), device_id_type=MESH)

    each(15, greet)
    pl.semaphore_signal(barrier, inc=1, device_id=(s_prev, e), device_id_type=MESH)
    pl.semaphore_wait(barrier, 16)

    def remote(src, dst, ss, rs, section, device):
        return pltpu.make_async_remote_copy(
            src_ref=src,
            dst_ref=dst,
            send_sem=ss,
            recv_sem=rs,
            device_id=(section, device),
            device_id_type=MESH,
        )

    def acts_copy(i, device, slot):
        return remote(
            acts.at[0, :, :, lanes(device, SLICE)], acts_in.at[slot], acts_ss.at[i], acts_rs.at[i], s, device
        )

    def down_copy(i, device, slot):
        return remote(
            down.at[0, :, :, lanes(device, SLICE)], down_in.at[slot], down_ss.at[i], down_rs.at[i], s, device
        )

    def up_copy(i, device, slot):
        return remote(up.at[0, :, :, lanes(device, SLICE)], up_in.at[slot], up_ss.at[i], up_rs.at[i], s, device)

    def meta_copy(i, device, slot):
        return remote(meta.at[slot], meta.at[slot], meta_ss.at[i], meta_rs.at[i], s, device)

    def part_copy(i, device, slot):
        return remote(
            part.at[lax.rem(device, 2), :, lanes(device // 2, BLOCK)],
            red.at[slot],
            part_ss.at[i],
            part_rs.at[i],
            s,
            device,
        )

    def low_copy(i, device, slot):
        return remote(low.at[slot], low.at[slot], low_ss.at[i], low_rs.at[i], s, device)

    def out_copy(i, device, slot):
        return remote(
            send_out.at[device], hand.at[slot], out_ss.at[i], out_rs.at[i], s, device
        )

    def hand_copy(i, slot):
        return remote(
            hand.at[slot],
            out.at[0, :, :, lanes(slot, SLICE)],
            hand_ss.at[i],
            hand_rs.at[i],
            s_next,
            e,
        )

    own = pltpu.make_async_copy(acts.at[0], own_acts, local_sem.at[0])
    own.start()

    def send_acts_down(i):
        acts_copy(i, peer(i), e).start()

    each(15, send_acts_down)

    def send_down(i):
        down_copy(i, peer(i), e).start()

    each(15, send_down)
    locals_ = [
        pltpu.make_async_copy(acts.at[0, :, :, lanes(e, SLICE)], acts_in.at[e], local_sem.at[1]),
        pltpu.make_async_copy(down.at[0, :, :, lanes(e, SLICE)], down_in.at[e], local_sem.at[2]),
        pltpu.make_async_copy(up.at[0, :, :, lanes(e, SLICE)], up_in.at[e], local_sem.at[3]),
    ]
    for copy in locals_:
        copy.start()

    own.wait()
    rows = MB * TOK

    def square(k, total):
        block = own_acts[:, :, lanes(k, SLICE)].astype(F32).reshape(rows, SLICE)
        return total + block * block

    squares = lax.fori_loop(0, GROUP, square, jnp.zeros((rows, SLICE), F32))
    inverse = lax.rsqrt(jnp.sum(squares, axis=1, keepdims=True) * (1.0 / WIDTH) + 1e-05)
    logits = scores[0].reshape(rows, 2)
    chosen = index[0].reshape(rows, 2).astype(F32)
    first = inverse / (1.0 + jnp.exp(logits[:, 1:2] - logits[:, 0:1]))
    second = inverse / (1.0 + jnp.exp(logits[:, 0:1] - logits[:, 1:2]))
    column = lax.broadcasted_iota(jnp.int32, (rows, 128), 1)
    table = jnp.where(
        column == 0,
        chosen[:, 0:1],
        jnp.where(
            column == 1,
            chosen[:, 1:2],
            jnp.where(column == 2, first, jnp.where(column == 3, second, 0.0)),
        ),
    )
    flat[...] = jnp.zeros_like(flat)
    flat[pl.ds(pl.multiple_of(c * rows, rows), rows), :] = table
    meta[e] = jnp.transpose(flat[...])[0:8]

    def send_meta(i):
        meta_copy(i, peer(i), e).start()

    each(15, send_meta)

    def send_up(i):
        up_copy(i, peer(i), e).start()

    each(15, send_up)

    for copy in locals_:
        copy.wait()

    def take(copy):
        def body(i):
            copy(i, source(i), source(i)).wait_recv()

        return body

    def receive(copy, dev_dependent=True):
        def body(i):
            copy(i, peer(i), source(i)).wait_recv()

        each(15, body)

    receive(acts_copy)
    receive(down_copy)
    receive(meta_copy)

    gain_row = gain[0:1, lanes(e, SLICE)]

    def down_step(n, carry):
        tokens = acts_in[pl.ds(n * 4, 4)].reshape(256, SLICE).astype(F32)
        scaled = (tokens * gain_row).astype(BF16)
        ids = []
        for k in range(2):
            parts = []
            for h in range(2):
                both = meta[4 * n + 2 * h] + meta[4 * n + 2 * h + 1]
                parts.append(both[k : k + 1])
            ids.append(jnp.concatenate(parts, axis=1))
        picked = [jnp.zeros((RANK, 256), F32) for _ in range(2)]
        for m in range(4):
            block = down_in[4 * m : 4 * m + 4].reshape(256, SLICE)
            product = lax.dot_general(
                block, scaled, (((1,), (1,)), ((), ())), preferred_element_type=F32
            )
            for g in range(16):
                piece = product[g * RANK : (g + 1) * RANK]
                expert = float(m * 16 + g)
                for k in range(2):
                    picked[k] = jnp.where(ids[k] == expert, piece, picked[k])
        for k in range(2):
            part[k, :, lanes(n, 256)] = picked[k]
        return carry

    lax.fori_loop(0, 4, down_step, 0)

    def send_part(i):
        part_copy(i, peer(i), e).start()

    each(15, send_part)
    red[e] = part[c, :, lanes(z, BLOCK)]
    receive(part_copy)

    total = red[0]
    for k in range(1, GROUP):
        total = total + red[k]
    both = meta[2 * z] + meta[2 * z + 1]
    factor = jnp.where(c == 0, both[2:3], both[3:4])
    low[e] = (total * factor).astype(BF16)

    def send_low(i):
        low_copy(i, peer(i), e).start()

    each(15, send_low)
    receive(low_copy)

    def mix_step(q, carry):
        both = meta[2 * q] + meta[2 * q + 1]
        lows = [low[2 * q].astype(F32), low[2 * q + 1].astype(F32)]
        for g in range(8):
            pieces = []
            for h in range(8):
                expert = float(g * 8 + h)
                piece = jnp.where(both[1:2] == expert, lows[1], 0.0)
                pieces.append(jnp.where(both[0:1] == expert, lows[0], piece))
            square_block = jnp.concatenate(pieces, axis=0)
            mixed[q, :, g * 128 : (g + 1) * 128] = jnp.transpose(square_block).astype(BF16)
        return carry

    lax.fori_loop(0, CHIPS, mix_step, 0)

    receive(up_copy)

    def out_block(q):
        weights = up_in[...].reshape(GROUP * LOCAL_EXPERTS * RANK, SLICE)
        delta = jnp.dot(mixed[q], weights, preferred_element_type=F32)
        base = acts_in[pl.ds(2 * q, 2)].reshape(BLOCK, SLICE).astype(F32)
        send_out[pl.ds(2 * q, 2)] = (base + delta).astype(BF16).reshape(2, MB, TOK, SLICE)

    def forward(i):
        out_copy(i, peer(i), source(i)).wait_recv()
        hand_copy(i, source(i)).start()

    def out_step(j, carry):
        out_block(lax.rem(z + hop(j), CHIPS))
        out_copy(2 * j, peer(2 * j), e).start()
        out_copy(2 * j + 1, peer(2 * j + 1), e).start()
        return carry

    def out_forward_step(j, carry):
        out_step(j, carry)
        forward(2 * j - 4)
        forward(2 * j - 3)
        return carry

    lax.fori_loop(0, 2, out_step, 0)
    lax.fori_loop(2, 7, out_forward_step, 0)
    out_block(z)
    out_copy(14, peer(14), e).start()
    own_hand = remote(
        send_out.at[e], out.at[0, :, :, lanes(e, SLICE)], hand_ss.at[15], hand_rs.at[15], s_next, e
    )
    own_hand.start()
    lax.fori_loop(10, 15, lambda i, carry: (forward(i), carry)[1], 0)

    def drain(i):
        acts_copy(i, peer(i), e).wait_send()
        down_copy(i, peer(i), e).wait_send()
        up_copy(i, peer(i), e).wait_send()
        meta_copy(i, peer(i), e).wait_send()
        part_copy(i, peer(i), e).wait_send()
        low_copy(i, peer(i), e).wait_send()
        out_copy(i, peer(i), e).wait_send()
        hand_copy(i, source(i)).wait()

    each(15, drain)
    own_hand.wait()


def local(acts, index, scores, gain, down, up):
    dma = pltpu.SemaphoreType.DMA((16,))
    any_spec = pl.BlockSpec(memory_space=pl.ANY)
    vmem_spec = pl.BlockSpec(memory_space=pltpu.VMEM)
    return pl.pallas_call(
        kernel,
        out_shape=jax.ShapeDtypeStruct(acts.shape, acts.dtype),
        in_specs=[any_spec, vmem_spec, vmem_spec, vmem_spec, any_spec, any_spec],
        out_specs=any_spec,
        scratch_shapes=[
            pltpu.VMEM((MB, TOK, WIDTH), BF16),
            pltpu.VMEM((GROUP, MB, TOK, SLICE), BF16),
            pltpu.VMEM((GROUP, LOCAL_EXPERTS, RANK, SLICE), BF16),
            pltpu.VMEM((GROUP, LOCAL_EXPERTS, RANK, SLICE), BF16),
            pltpu.VMEM((128, 128), F32),
            pltpu.VMEM((GROUP, 8, 128), F32),
            pltpu.VMEM((2, RANK, GROUP * MB * TOK), F32),
            pltpu.VMEM((GROUP, RANK, BLOCK), F32),
            pltpu.VMEM((GROUP, RANK, BLOCK), BF16),
            pltpu.VMEM((CHIPS, BLOCK, GROUP * LOCAL_EXPERTS * RANK), BF16),
            pltpu.VMEM((GROUP, MB, TOK, SLICE), BF16),
            pltpu.VMEM((GROUP, MB, TOK, SLICE), BF16),
        ]
        + [dma] * 17,
        compiler_params=pltpu.CompilerParams(
            collective_id=0, has_side_effects=True, vmem_limit_bytes=40 << 20
        ),
        cost_estimate=pl.CostEstimate(
            flops=4 * 1024 * 1024 * SLICE, bytes_accessed=4 * 786432, transcendentals=0
        ),
        name="relay",
    )(acts, index, scores, gain, down, up)


def solution(mesh):
    return jax.shard_map(
        local,
        mesh=mesh,
        in_specs=(
            P("section", None, "expert", None),
            P("section", None, "expert", None),
            P("section", None, "expert", None),
            P("section", None),
            P("section", "expert", None, None),
            P("section", "expert", None, None),
        ),
        out_specs=P("section", None, "expert", None),
        check_vma=False,
    )
```

```python
import jax
import jax.numpy as jnp
from jax import lax
from jax.experimental import pallas as pl
from jax.experimental.pallas import tpu as pltpu
from jax.sharding import PartitionSpec as P

MESH = pl.DeviceIdType.MESH
SECTIONS = 32
CHIPS = 8
GROUP = 16
MB = 2
TOK = 32
ROWS = MB * TOK
RANK = 16
LOCAL_EXPERTS = 4
EXPERTS = GROUP * LOCAL_EXPERTS
WIDTH = 6144
SLICE = WIDTH // GROUP
LANES = 128
PARTS = SLICE // LANES
BLOCK = 2 * ROWS
ORDER = (
    (4, 1), (1, 0), (7, 0), (3, 1), (5, 1), (2, 0), (6, 0), (4, 0),
    (3, 0), (5, 0), (1, 1), (7, 1), (2, 1), (6, 1), (0, 1),
)
NEAR = (0, 1, 7, 2, 6, 3, 5, 4)
WINDOW = 8
PAIRS = ((0, 1), (7, 2), (6, 3), (5, 4))
F32 = jnp.float32
BF16 = jnp.bfloat16


def kernel(
    acts,
    index,
    scores,
    gain,
    down,
    up,
    out,
    own_acts,
    acts_in,
    down_in,
    up_in,
    gain_in,
    index_in,
    scores_in,
    place,
    flat,
    ids_in,
    gates_in,
    part,
    red,
    low,
    mixed,
    send_out,
    hand,
    local_sem,
    acts_ss,
    acts_rs,
    down_ss,
    down_rs,
    up_ss,
    up_rs,
    ids_ss,
    ids_rs,
    gates_ss,
    gates_rs,
    part_ss,
    part_rs,
    low_ss,
    low_rs,
    out_ss,
    out_rs,
    hand_ss,
    hand_rs,
):
    s = lax.axis_index("section")
    e = lax.axis_index("expert")
    z = e // 2
    c = lax.rem(e, 2)
    sibling = 2 * z + 1 - c
    s_next = lax.rem(s + 1, SECTIONS)
    s_prev = lax.rem(s + SECTIONS - 1, SECTIONS)

    others = [lax.rem(z + hops, CHIPS) * 2 + lax.rem(c + flip, 2) for hops, flip in ORDER]
    arrivals = [sibling]
    for hops in NEAR[1:]:
        other = lax.rem(z + hops, CHIPS) * 2
        arrivals += [other + 1 - c, other + c]

    def span(k, width):
        return pl.ds(pl.multiple_of(k * width, width), width)

    def piece(device, g):
        return pl.ds(pl.multiple_of(device * SLICE + g * LANES, LANES), LANES)

    def each(count, body):
        def step(i, carry):
            body(i)
            return carry

        lax.fori_loop(0, count, step, 0)

    def peers(body):
        for device in others:
            body(device)

    barrier = pltpu.get_barrier_semaphore()

    def greet(device):
        pl.semaphore_signal(barrier, inc=1, device_id=(s, device), device_id_type=MESH)

    peers(greet)
    pl.semaphore_signal(barrier, inc=1, device_id=(s_prev, e), device_id_type=MESH)

    early = [
        pltpu.make_async_copy(acts, own_acts, local_sem.at[0]),
        pltpu.make_async_copy(index.at[0], index_in, local_sem.at[1]),
        pltpu.make_async_copy(scores.at[0], scores_in, local_sem.at[2]),
    ]
    late = [
        pltpu.make_async_copy(gain.at[:, span(e, SLICE)], gain_in, local_sem.at[3]),
        pltpu.make_async_copy(acts.at[:, span(e, SLICE)], acts_in.at[e], local_sem.at[4]),
        pltpu.make_async_copy(down.at[:, span(e, SLICE)], down_in.at[e], local_sem.at[5]),
    ]
    for g in range(PARTS):
        late.append(pltpu.make_async_copy(up.at[:, piece(e, g)], up_in.at[g, e], local_sem.at[6 + g]))
    for copy in early + late:
        copy.start()
    place[...] = jnp.zeros_like(place)
    flat[...] = jnp.zeros_like(flat)

    for copy in early:
        copy.wait()
    for m in range(MB):
        place[m, 0:2, 0:TOK] = index_in[m].astype(F32)
        place[m, 2:4, 0:TOK] = scores_in[m]
    placed = pltpu.roll(place[0], c * ROWS, 1) + pltpu.roll(place[1], c * ROWS + TOK, 1)
    ids_in[e] = placed[0:2]

    def square(k, total):
        block = own_acts[:, span(k, SLICE)].astype(F32)
        return total + block * block

    squares = lax.fori_loop(0, GROUP, square, jnp.zeros((ROWS, SLICE), F32))
    inverse = lax.rsqrt(jnp.sum(squares, axis=1, keepdims=True) * (1.0 / WIDTH) + 1e-05)
    flat[span(c, ROWS), :] = jnp.broadcast_to(inverse, (ROWS, LANES))
    inverse_row = jnp.transpose(flat[...])[0:1]
    first = inverse_row / (1.0 + jnp.exp(placed[3:4] - placed[2:3]))
    second = inverse_row / (1.0 + jnp.exp(placed[2:3] - placed[3:4]))
    gates_in[c] = jnp.concatenate([first, second], axis=0)
    pl.semaphore_wait(barrier, GROUP)

    def remote(src, dst, ss, rs, section, device):
        return pltpu.make_async_remote_copy(
            src_ref=src,
            dst_ref=dst,
            send_sem=ss,
            recv_sem=rs,
            device_id=(section, device),
            device_id_type=MESH,
        )

    def acts_copy(device, slot):
        src = acts.at[:, span(device, SLICE)]
        return remote(src, acts_in.at[slot], acts_ss.at[device], acts_rs.at[slot], s, device)

    def down_copy(device, slot):
        src = down.at[:, span(device, SLICE)]
        return remote(src, down_in.at[slot], down_ss.at[device], down_rs.at[slot], s, device)

    def up_copy(g):
        def copy(device, slot):
            src = up.at[:, piece(device, g)]
            return remote(src, up_in.at[g, slot], up_ss.at[g, device], up_rs.at[g, slot], s, device)

        return copy

    def ids_copy(device, slot):
        return remote(ids_in.at[slot], ids_in.at[slot], ids_ss.at[device], ids_rs.at[slot], s, device)

    def gates_copy(slot):
        return remote(
            gates_in.at[slot], gates_in.at[slot], gates_ss, gates_rs, s, sibling
        )

    def part_copy(device, slot):
        src = part.at[lax.rem(device, 2), :, span(device // 2, BLOCK)]
        return remote(src, red.at[slot], part_ss.at[device], part_rs.at[slot], s, device)

    def low_copy(device, slot):
        return remote(low.at[slot], low.at[slot], low_ss.at[device], low_rs.at[slot], s, device)

    def out_copy(g):
        def copy(device, slot):
            return remote(
                send_out.at[g, device], hand.at[g, slot], out_ss.at[g, device], out_rs.at[g, slot], s, device
            )

        return copy

    def hand_copy(g, slot, own):
        src = send_out if own else hand
        return remote(
            src.at[g, slot],
            out.at[:, piece(slot, g)],
            hand_ss.at[g, slot],
            hand_rs.at[g, slot],
            s_next,
            e,
        )

    def send(copy):
        peers(lambda device: copy(device, e).start())

    def sent(copy):
        peers(lambda device: copy(device, e).wait_send())

    def received(copy):
        peers(lambda device: copy(device, device).wait_recv())

    gates_copy(c).start()
    send(ids_copy)
    bulk = [acts_copy(device, e) for device in others] + [down_copy(device, e) for device in others]
    for k, copy in enumerate(bulk):
        if k >= WINDOW:
            bulk[k - WINDOW].wait_send()
        copy.start()
    G0 = 3
    for k, copy in enumerate(bulk[-WINDOW:]):
        copy.wait_send()
        for device in others[G0 * k : G0 * (k + 1)]:
            up_copy(0)(device, e).start()
    for device in others[G0 * WINDOW :]:
        up_copy(0)(device, e).start()


    for copy in late:
        copy.wait()
    received(ids_copy)
    received(acts_copy)
    received(down_copy)

    def pick_block(n):
        tokens = acts_in[span(n, 4)].reshape(2 * BLOCK, SLICE).astype(F32)
        scaled = (tokens * gain_in[...]).astype(BF16)
        halves = [ids_in[4 * n + 2 * h] + ids_in[4 * n + 2 * h + 1] for h in range(2)]
        both = jnp.concatenate(halves, axis=1)
        picked = [jnp.zeros((RANK, 2 * BLOCK), F32) for _ in range(2)]
        for m in range(4):
            block = down_in[4 * m : 4 * m + 4].reshape(256, SLICE)
            product = lax.dot_general(block, scaled, (((1,), (1,)), ((), ())), preferred_element_type=F32)
            for g in range(16):
                rows = product[g * RANK : (g + 1) * RANK]
                for k in range(2):
                    picked[k] = jnp.where(both[k : k + 1] == float(m * 16 + g), rows, picked[k])
        for k in range(2):
            part[k, :, span(n, 2 * BLOCK)] = picked[k]

    def pick_step(i):
        n = lax.rem(z // 2 + 1 + i, 4)
        pick_block(n)
        for h in range(4):
            part_copy(4 * n + h, e).start()

    each(3, pick_step)
    pick_block(z // 2)
    chip = z + 1 - 2 * lax.rem(z, 2)
    part_copy(2 * chip, e).start()
    part_copy(2 * chip + 1, e).start()
    part_copy(sibling, e).start()
    red[e] = part[c, :, span(z, BLOCK)]
    send(up_copy(1))
    received(part_copy)
    gates_copy(1 - c).wait_recv()

    total = red[0]
    for k in range(1, GROUP):
        total = total + red[k]
    gates = gates_in[0] + gates_in[1]
    low[e] = (total * jnp.where(c == 0, gates[0:1], gates[1:2])).astype(BF16)
    send(low_copy)
    send(up_copy(2))
    received(low_copy)


    def mix_step(q):
        both = ids_in[2 * q] + ids_in[2 * q + 1]
        lows = [low[2 * q].astype(F32), low[2 * q + 1].astype(F32)]
        for g in range(8):
            pieces = []
            for h in range(8):
                expert = float(g * 8 + h)
                rows = jnp.where(both[1:2] == expert, lows[1], 0.0)
                pieces.append(jnp.where(both[0:1] == expert, lows[0], rows))
            tile = jnp.concatenate(pieces, axis=0)
            mixed[q, :, g * LANES : (g + 1) * LANES] = jnp.transpose(tile).astype(BF16)

    each(CHIPS, mix_step)

    def out_part(g):
        received(up_copy(g))
        weights = up_in[g].reshape(EXPERTS * RANK, LANES)
        for pair in PAIRS:
            chips = [lax.rem(z + hops, CHIPS) for hops in pair]
            rows = jnp.concatenate([mixed[q] for q in chips], axis=0)
            delta = jnp.dot(rows, weights, preferred_element_type=F32)
            for k, q in enumerate(chips):
                base = acts_in[span(q, 2), :, span(g, LANES)].reshape(BLOCK, LANES).astype(F32)
                mine = delta[k * BLOCK : (k + 1) * BLOCK]
                send_out[g, span(q, 2)] = (base + mine).astype(BF16).reshape(2, ROWS, LANES)
            for hops, q in zip(pair, chips):
                if hops == 0:
                    out_copy(g)(sibling, e).start()
                    hand_copy(g, e, True).start()
                else:
                    out_copy(g)(2 * q + 1 - c, e).start()
                    out_copy(g)(2 * q + c, e).start()


    def forward(g, devices):
        for device in devices:
            out_copy(g)(device, device).wait_recv()
            hand_copy(g, device, False).start()

    out_part(0)
    forward(0, arrivals[:5])
    out_part(1)
    forward(0, arrivals[5:])
    out_part(2)
    forward(1, arrivals)
    forward(2, arrivals)

    def drain_part(g):
        sent(up_copy(g))
        sent(out_copy(g))
        peers(lambda device: hand_copy(g, device, False).wait())
        hand_copy(g, e, True).wait()

    sent(ids_copy)
    gates_copy(c).wait_send()
    sent(part_copy)
    sent(low_copy)
    each(PARTS, drain_part)


def local(acts, index, scores, gain, down, up):
    dma = pltpu.SemaphoreType.DMA
    space = pl.BlockSpec(memory_space=pl.ANY)
    return pl.pallas_call(
        kernel,
        out_shape=jax.ShapeDtypeStruct((ROWS, WIDTH), acts.dtype),
        in_specs=[pl.BlockSpec(memory_space=pltpu.HBM)] * 6,
        out_specs=space,
        scratch_shapes=[
            pltpu.VMEM((ROWS, WIDTH), BF16),
            pltpu.VMEM((GROUP, ROWS, SLICE), BF16),
            pltpu.VMEM((GROUP, ROWS, SLICE), BF16),
            pltpu.VMEM((PARTS, GROUP, ROWS, LANES), BF16),
            pltpu.VMEM((1, SLICE), F32),
            pltpu.VMEM((MB, 2, TOK), jnp.int32),
            pltpu.VMEM((MB, 2, TOK), F32),
            pltpu.VMEM((MB, 8, LANES), F32),
            pltpu.VMEM((LANES, LANES), F32),
            pltpu.VMEM((GROUP, 2, LANES), F32),
            pltpu.VMEM((2, 2, LANES), F32),
            pltpu.VMEM((2, RANK, GROUP * ROWS), F32),
            pltpu.VMEM((GROUP, RANK, BLOCK), F32),
            pltpu.VMEM((GROUP, RANK, BLOCK), BF16),
            pltpu.VMEM((CHIPS, BLOCK, EXPERTS * RANK), BF16),
            pltpu.VMEM((PARTS, GROUP, ROWS, LANES), BF16),
            pltpu.VMEM((PARTS, GROUP, ROWS, LANES), BF16),
            dma((9,)),
        ]
        + [dma((GROUP,))] * 4
        + [dma((PARTS, GROUP))] * 2
        + [dma((GROUP,))] * 2
        + [dma] * 2
        + [dma((GROUP,))] * 4
        + [dma((PARTS, GROUP))] * 4,
        compiler_params=pltpu.CompilerParams(
            collective_id=0, has_side_effects=True, vmem_limit_bytes=60 << 20
        ),
        cost_estimate=pl.CostEstimate(
            flops=4 * 1024 * 1024 * SLICE, bytes_accessed=4 * 786432, transcendentals=0
        ),
        name="relay",
    )(
        acts.reshape(ROWS, WIDTH),
        jnp.swapaxes(index, 2, 3),
        jnp.swapaxes(scores, 2, 3),
        gain,
        down.reshape(ROWS, WIDTH),
        up.reshape(ROWS, WIDTH),
    ).reshape(acts.shape)


def solution(mesh):
    return jax.shard_map(
        local,
        mesh=mesh,
        in_specs=(
            P("section", None, "expert", None),
            P("section", None, "expert", None),
            P("section", None, "expert", None),
            P("section", None),
            P("section", "expert", None, None),
            P("section", "expert", None, None),
        ),
        out_specs=P("section", None, "expert", None),
        check_vma=False,
    )
```

```python
import jax
import jax.numpy as jnp
from jax import lax
from jax.experimental import pallas as pl
from jax.experimental.pallas import tpu as pltpu
from jax.sharding import PartitionSpec as P

MESH = pl.DeviceIdType.MESH
SECTIONS = 32
CHIPS = 8
GROUP = 16
MB = 2
TOK = 32
ROWS = MB * TOK
RANK = 16
LOCAL_EXPERTS = 4
EXPERTS = GROUP * LOCAL_EXPERTS
WIDTH = 6144
SLICE = WIDTH // GROUP
LANES = 128
PARTS = SLICE // LANES
BLOCK = 2 * ROWS
ORDER = (
    (4, 1), (1, 0), (7, 0), (3, 1), (5, 1), (2, 0), (6, 0), (4, 0),
    (3, 0), (5, 0), (1, 1), (7, 1), (2, 1), (6, 1), (0, 1),
)
NEAR = (0, 1, 7, 2, 6, 3, 5, 4)
WINDOW = 8
PAIRS = ((0, 1), (7, 2), (6, 3), (5, 4))
F32 = jnp.float32
BF16 = jnp.bfloat16


def kernel(
    acts,
    index,
    scores,
    gain,
    down,
    up,
    out,
    own_acts,
    acts_in,
    down_in,
    up_in,
    gain_in,
    index_in,
    scores_in,
    place,
    flat,
    ids_in,
    gates_in,
    part,
    red,
    low,
    mixed,
    mixed_prev,
    acts_prev,
    up_prev,
    ids_prev,
    low_prev,
    send_out,
    hand,
    local_sem,
    acts_ss,
    acts_rs,
    down_ss,
    down_rs,
    up_ss,
    up_rs,
    ids_ss,
    ids_rs,
    gates_ss,
    gates_rs,
    part_ss,
    part_rs,
    low_ss,
    low_rs,
    out_ss,
    out_rs,
    hand_ss,
    hand_rs,
    next_ss,
    next_rs,
):
    s = lax.axis_index("section")
    e = lax.axis_index("expert")
    z = e // 2
    c = lax.rem(e, 2)
    sibling = 2 * z + 1 - c
    s_next = lax.rem(s + 1, SECTIONS)
    s_prev = lax.rem(s + SECTIONS - 1, SECTIONS)

    others = [lax.rem(z + hops, CHIPS) * 2 + lax.rem(c + flip, 2) for hops, flip in ORDER]

    def span(k, width):
        return pl.ds(pl.multiple_of(k * width, width), width)

    def piece(device, g):
        return pl.ds(pl.multiple_of(device * SLICE + g * LANES, LANES), LANES)

    def each(count, body):
        def step(i, carry):
            body(i)
            return carry

        lax.fori_loop(0, count, step, 0)

    def peers(body):
        for device in others:
            body(device)

    barrier = pltpu.get_barrier_semaphore()

    def greet(device):
        pl.semaphore_signal(barrier, inc=1, device_id=(s, device), device_id_type=MESH)

    peers(greet)
    pl.semaphore_signal(barrier, inc=1, device_id=(s_prev, e), device_id_type=MESH)

    early = [
        pltpu.make_async_copy(acts, own_acts, local_sem.at[0]),
        pltpu.make_async_copy(index.at[0], index_in, local_sem.at[1]),
        pltpu.make_async_copy(scores.at[0], scores_in, local_sem.at[2]),
    ]
    late = [
        pltpu.make_async_copy(gain.at[:, span(e, SLICE)], gain_in, local_sem.at[3]),
        pltpu.make_async_copy(acts.at[:, span(e, SLICE)], acts_in.at[e], local_sem.at[4]),
        pltpu.make_async_copy(down.at[:, span(e, SLICE)], down_in.at[e], local_sem.at[5]),
    ]
    for g in range(PARTS):
        late.append(pltpu.make_async_copy(up.at[:, piece(e, g)], up_in.at[g, e], local_sem.at[6 + g]))
    for copy in early + late:
        copy.start()
    place[...] = jnp.zeros_like(place)
    flat[...] = jnp.zeros_like(flat)

    for copy in early:
        copy.wait()
    for m in range(MB):
        place[m, 0:2, 0:TOK] = index_in[m].astype(F32)
        place[m, 2:4, 0:TOK] = scores_in[m]
    placed = pltpu.roll(place[0], c * ROWS, 1) + pltpu.roll(place[1], c * ROWS + TOK, 1)
    ids_in[e] = placed[0:2]

    def square(k, total):
        block = own_acts[:, span(k, SLICE)].astype(F32)
        return total + block * block

    squares = lax.fori_loop(0, GROUP, square, jnp.zeros((ROWS, SLICE), F32))
    inverse = lax.rsqrt(jnp.sum(squares, axis=1, keepdims=True) * (1.0 / WIDTH) + 1e-05)
    flat[span(c, ROWS), :] = jnp.broadcast_to(inverse, (ROWS, LANES))
    inverse_row = jnp.transpose(flat[...])[0:1]
    first = inverse_row / (1.0 + jnp.exp(placed[3:4] - placed[2:3]))
    second = inverse_row / (1.0 + jnp.exp(placed[2:3] - placed[3:4]))
    gates_in[c] = jnp.concatenate([first, second], axis=0)
    pl.semaphore_wait(barrier, GROUP)

    def remote(src, dst, ss, rs, section, device):
        return pltpu.make_async_remote_copy(
            src_ref=src,
            dst_ref=dst,
            send_sem=ss,
            recv_sem=rs,
            device_id=(section, device),
            device_id_type=MESH,
        )

    def acts_copy(device, slot):
        src = acts.at[:, span(device, SLICE)]
        return remote(src, acts_in.at[slot], acts_ss.at[device], acts_rs.at[slot], s, device)

    def down_copy(device, slot):
        src = down.at[:, span(device, SLICE)]
        return remote(src, down_in.at[slot], down_ss.at[device], down_rs.at[slot], s, device)

    def up_copy(g):
        def copy(device, slot):
            src = up.at[:, piece(device, g)]
            return remote(src, up_in.at[g, slot], up_ss.at[g, device], up_rs.at[g, slot], s, device)

        return copy

    def ids_copy(device, slot):
        return remote(ids_in.at[slot], ids_in.at[slot], ids_ss.at[device], ids_rs.at[slot], s, device)

    def gates_copy(slot):
        return remote(
            gates_in.at[slot], gates_in.at[slot], gates_ss, gates_rs, s, sibling
        )

    def part_copy(device, slot):
        src = part.at[lax.rem(device, 2), :, span(device // 2, BLOCK)]
        return remote(src, red.at[slot], part_ss.at[device], part_rs.at[slot], s, device)

    def low_copy(device, slot):
        return remote(low.at[slot], low.at[slot], low_ss.at[device], low_rs.at[slot], s, device)

    def out_copy(g):
        def copy(device, slot):
            return remote(
                send_out.at[g, device], hand.at[g, slot], out_ss.at[g, device], out_rs.at[g, slot], s, device
            )

        return copy

    def hand_copy(g, slot, own):
        src = send_out if own else hand
        return remote(
            src.at[g, slot],
            out.at[:, piece(slot, g)],
            hand_ss.at[g, slot],
            hand_rs.at[g, slot],
            s_next,
            e,
        )

    def next_copy(k):
        src, dst = (
            (acts_in.at[:, :, pl.ds(0, LANES)], acts_prev),
            (ids_in, ids_prev),
            (up_in.at[0], up_prev),
            (low, low_prev),
        )[k]
        return remote(src, dst, next_ss.at[k], next_rs.at[k], s_next, e)

    def last_copy(device, slot):
        return remote(
            send_out.at[0, device], out.at[:, piece(slot, 0)], out_ss.at[0, device], out_rs.at[0, slot], s, device
        )

    def send(copy):
        peers(lambda device: copy(device, e).start())

    def sent(copy):
        peers(lambda device: copy(device, e).wait_send())

    def received(copy):
        peers(lambda device: copy(device, device).wait_recv())

    gates_copy(c).start()
    send(ids_copy)
    bulk = [acts_copy(device, e) for device in others] + [down_copy(device, e) for device in others]
    for k, copy in enumerate(bulk):
        if k >= WINDOW:
            bulk[k - WINDOW].wait_send()
        copy.start()
    G0 = 3
    for k, copy in enumerate(bulk[-WINDOW:]):
        copy.wait_send()
        for device in others[G0 * k : G0 * (k + 1)]:
            up_copy(0)(device, e).start()
    for device in others[G0 * WINDOW :]:
        up_copy(0)(device, e).start()


    for copy in late:
        copy.wait()
    received(ids_copy)
    next_copy(1).start()
    received(acts_copy)
    next_copy(0).start()
    received(down_copy)

    def pick_block(n):
        tokens = acts_in[span(n, 4)].reshape(2 * BLOCK, SLICE).astype(F32)
        scaled = (tokens * gain_in[...]).astype(BF16)
        halves = [ids_in[4 * n + 2 * h] + ids_in[4 * n + 2 * h + 1] for h in range(2)]
        both = jnp.concatenate(halves, axis=1)
        picked = [jnp.zeros((RANK, 2 * BLOCK), F32) for _ in range(2)]
        for m in range(4):
            block = down_in[4 * m : 4 * m + 4].reshape(256, SLICE)
            product = lax.dot_general(block, scaled, (((1,), (1,)), ((), ())), preferred_element_type=F32)
            for g in range(16):
                rows = product[g * RANK : (g + 1) * RANK]
                for k in range(2):
                    picked[k] = jnp.where(both[k : k + 1] == float(m * 16 + g), rows, picked[k])
        for k in range(2):
            part[k, :, span(n, 2 * BLOCK)] = picked[k]

    def pick_step(i):
        n = lax.rem(z // 2 + 1 + i, 4)
        pick_block(n)
        for h in range(4):
            part_copy(4 * n + h, e).start()

    each(3, pick_step)
    pick_block(z // 2)
    chip = z + 1 - 2 * lax.rem(z, 2)
    part_copy(2 * chip, e).start()
    part_copy(2 * chip + 1, e).start()
    part_copy(sibling, e).start()
    red[e] = part[c, :, span(z, BLOCK)]
    send(up_copy(1))
    received(up_copy(0))
    next_copy(2).start()
    received(part_copy)
    gates_copy(1 - c).wait_recv()

    total = red[0]
    for k in range(1, GROUP):
        total = total + red[k]
    gates = gates_in[0] + gates_in[1]
    low[e] = (total * jnp.where(c == 0, gates[0:1], gates[1:2])).astype(BF16)
    send(low_copy)
    send(up_copy(2))
    received(low_copy)
    next_copy(3).start()


    def mix(ids, lows_in, result):
        def mix_step(q):
            both = ids[2 * q] + ids[2 * q + 1]
            lows = [lows_in[2 * q].astype(F32), lows_in[2 * q + 1].astype(F32)]
            for g in range(8):
                pieces = []
                for h in range(8):
                    expert = float(g * 8 + h)
                    rows = jnp.where(both[1:2] == expert, lows[1], 0.0)
                    pieces.append(jnp.where(both[0:1] == expert, lows[0], rows))
                tile = jnp.concatenate(pieces, axis=0)
                result[q, :, g * LANES : (g + 1) * LANES] = jnp.transpose(tile).astype(BF16)

        each(CHIPS, mix_step)

    def out_part(g, weights_in, table, base_in, start):
        weights = weights_in[...].reshape(EXPERTS * RANK, LANES)
        for pair in PAIRS:
            chips = [lax.rem(z + hops, CHIPS) for hops in pair]
            rows = jnp.concatenate([table[q] for q in chips], axis=0)
            delta = jnp.dot(rows, weights, preferred_element_type=F32)
            for k, (hops, q) in enumerate(zip(pair, chips)):
                base = base_in(q).reshape(BLOCK, LANES).astype(F32)
                mine = delta[k * BLOCK : (k + 1) * BLOCK]
                send_out[g, span(q, 2)] = (base + mine).astype(BF16).reshape(2, ROWS, LANES)
                if hops == 0:
                    start(sibling)
                else:
                    start(2 * q + 1 - c)
                    start(2 * q + c)

    def own_part(g):
        received(up_copy(g))
        out_part(
            g,
            up_in.at[g],
            mixed,
            lambda q: acts_in[span(q, 2), :, g * LANES : (g + 1) * LANES],
            lambda device: out_copy(g)(device, e).start(),
        )
        hand_copy(g, e, True).start()

    arrivals = [sibling]
    for hops in NEAR[1:]:
        other = lax.rem(z + hops, CHIPS) * 2
        arrivals += [other + 1 - c, other + c]

    def forward(g, devices):
        for device in devices:
            out_copy(g)(device, device).wait_recv()
            hand_copy(g, device, False).start()

    mix(ids_in, low, mixed)
    own_part(1)
    own_part(2)
    F1 = 5
    forward(1, arrivals[:F1])
    for k in range(4):
        next_copy(k).wait_recv()
    mix(ids_prev, low_prev, mixed_prev)
    out_part(
        0,
        up_prev,
        mixed_prev,
        lambda q: acts_prev[span(q, 2)],
        lambda device: last_copy(device, e).start(),
    )
    last = pltpu.make_async_copy(send_out.at[0, e], out.at[:, piece(e, 0)], local_sem.at[9])
    last.start()
    forward(1, arrivals[F1:])
    forward(2, arrivals)

    for g in range(1, PARTS):
        sent(out_copy(g))
        peers(lambda device: hand_copy(g, device, False).wait())
        hand_copy(g, e, True).wait()
    received(last_copy)
    sent(last_copy)
    last.wait()
    for k in range(4):
        next_copy(k).wait_send()
    for g in range(PARTS):
        sent(up_copy(g))
    gates_copy(c).wait_send()
    sent(ids_copy)
    sent(part_copy)
    sent(low_copy)


def local(acts, index, scores, gain, down, up):
    dma = pltpu.SemaphoreType.DMA
    space = pl.BlockSpec(memory_space=pl.ANY)
    return pl.pallas_call(
        kernel,
        out_shape=jax.ShapeDtypeStruct((ROWS, WIDTH), acts.dtype),
        in_specs=[pl.BlockSpec(memory_space=pltpu.HBM)] * 6,
        out_specs=space,
        scratch_shapes=[
            pltpu.VMEM((ROWS, WIDTH), BF16),
            pltpu.VMEM((GROUP, ROWS, SLICE), BF16),
            pltpu.VMEM((GROUP, ROWS, SLICE), BF16),
            pltpu.VMEM((PARTS, GROUP, ROWS, LANES), BF16),
            pltpu.VMEM((1, SLICE), F32),
            pltpu.VMEM((MB, 2, TOK), jnp.int32),
            pltpu.VMEM((MB, 2, TOK), F32),
            pltpu.VMEM((MB, 8, LANES), F32),
            pltpu.VMEM((LANES, LANES), F32),
            pltpu.VMEM((GROUP, 2, LANES), F32),
            pltpu.VMEM((2, 2, LANES), F32),
            pltpu.VMEM((2, RANK, GROUP * ROWS), F32),
            pltpu.VMEM((GROUP, RANK, BLOCK), F32),
            pltpu.VMEM((GROUP, RANK, BLOCK), BF16),
            pltpu.VMEM((CHIPS, BLOCK, EXPERTS * RANK), BF16),
            pltpu.VMEM((CHIPS, BLOCK, EXPERTS * RANK), BF16),
            pltpu.VMEM((GROUP, ROWS, LANES), BF16),
            pltpu.VMEM((GROUP, ROWS, LANES), BF16),
            pltpu.VMEM((GROUP, 2, LANES), F32),
            pltpu.VMEM((GROUP, RANK, BLOCK), BF16),
            pltpu.VMEM((PARTS, GROUP, ROWS, LANES), BF16),
            pltpu.VMEM((PARTS, GROUP, ROWS, LANES), BF16),
            dma((10,)),
        ]
        + [dma((GROUP,))] * 4
        + [dma((PARTS, GROUP))] * 2
        + [dma((GROUP,))] * 2
        + [dma] * 2
        + [dma((GROUP,))] * 4
        + [dma((PARTS, GROUP))] * 4
        + [dma((4,))] * 2,
        compiler_params=pltpu.CompilerParams(
            collective_id=0, has_side_effects=True, vmem_limit_bytes=60 << 20
        ),
        cost_estimate=pl.CostEstimate(
            flops=4 * 1024 * 1024 * SLICE, bytes_accessed=4 * 786432, transcendentals=0
        ),
        name="relay",
    )(
        acts.reshape(ROWS, WIDTH),
        jnp.swapaxes(index, 2, 3),
        jnp.swapaxes(scores, 2, 3),
        gain,
        down.reshape(ROWS, WIDTH),
        up.reshape(ROWS, WIDTH),
    ).reshape(acts.shape)


def solution(mesh):
    return jax.shard_map(
        local,
        mesh=mesh,
        in_specs=(
            P("section", None, "expert", None),
            P("section", None, "expert", None),
            P("section", None, "expert", None),
            P("section", None),
            P("section", "expert", None, None),
            P("section", "expert", None, None),
        ),
        out_specs=P("section", None, "expert", None),
        check_vma=False,
    )
```

```python
import jax
import jax.numpy as jnp
from jax import lax
from jax.experimental import pallas as pl
from jax.experimental.pallas import tpu as pltpu
from jax.sharding import PartitionSpec as P

MESH = pl.DeviceIdType.MESH
SECTIONS = 32
CHIPS = 8
GROUP = 16
MB = 2
TOK = 32
ROWS = MB * TOK
RANK = 16
LOCAL_EXPERTS = 4
EXPERTS = GROUP * LOCAL_EXPERTS
WIDTH = 6144
SLICE = WIDTH // GROUP
LANES = 128
PARTS = SLICE // LANES
BLOCK = 2 * ROWS
ORDER = (
    (4, 1), (4, 0), (3, 1), (3, 0), (5, 1), (5, 0), (2, 1), (2, 0),
    (6, 1), (6, 0), (1, 1), (1, 0), (7, 1), (7, 0), (0, 1),
)
NEAR = (0, 1, 7, 2, 6, 3, 5, 4)
PAIRS = ((0, 1), (7, 2), (6, 3), (5, 4))
F32 = jnp.float32
BF16 = jnp.bfloat16


def kernel(
    acts,
    index,
    scores,
    gain,
    down,
    up,
    out,
    own_acts,
    acts_in,
    down_in,
    up_in,
    gain_in,
    index_in,
    scores_in,
    place,
    flat,
    ids_in,
    gates_in,
    part,
    red,
    low,
    mixed,
    mixed_prev,
    acts_prev,
    up_prev,
    ids_prev,
    low_prev,
    send_out,
    hand,
    local_sem,
    acts_ss,
    acts_rs,
    down_ss,
    down_rs,
    up_ss,
    up_rs,
    ids_ss,
    ids_rs,
    gates_ss,
    gates_rs,
    part_ss,
    part_rs,
    low_ss,
    low_rs,
    out_ss,
    out_rs,
    hand_ss,
    hand_rs,
    next_ss,
    next_rs,
):
    s = lax.axis_index("section")
    e = lax.axis_index("expert")
    z = e // 2
    c = lax.rem(e, 2)
    sibling = 2 * z + 1 - c
    s_next = lax.rem(s + 1, SECTIONS)
    s_prev = lax.rem(s + SECTIONS - 1, SECTIONS)

    others = [lax.rem(z + hops, CHIPS) * 2 + lax.rem(c + flip, 2) for hops, flip in ORDER]

    def span(k, width):
        return pl.ds(pl.multiple_of(k * width, width), width)

    def piece(device, g):
        return pl.ds(pl.multiple_of(device * SLICE + g * LANES, LANES), LANES)

    def each(count, body):
        def step(i, carry):
            body(i)
            return carry

        lax.fori_loop(0, count, step, 0)

    def peers(body):
        for device in others:
            body(device)

    barrier = pltpu.get_barrier_semaphore()

    def greet(device):
        pl.semaphore_signal(barrier, inc=1, device_id=(s, device), device_id_type=MESH)

    peers(greet)
    pl.semaphore_signal(barrier, inc=1, device_id=(s_prev, e), device_id_type=MESH)

    early = [
        pltpu.make_async_copy(acts, own_acts, local_sem.at[0]),
        pltpu.make_async_copy(index.at[0], index_in, local_sem.at[1]),
        pltpu.make_async_copy(scores.at[0], scores_in, local_sem.at[2]),
    ]
    late = [
        pltpu.make_async_copy(gain.at[:, span(e, SLICE)], gain_in, local_sem.at[3]),
        pltpu.make_async_copy(acts.at[:, span(e, SLICE)], acts_in.at[e], local_sem.at[4]),
        pltpu.make_async_copy(down.at[:, span(e, SLICE)], down_in.at[e], local_sem.at[5]),
    ]
    for g in range(PARTS):
        late.append(pltpu.make_async_copy(up.at[:, piece(e, g)], up_in.at[g, e], local_sem.at[6 + g]))
    for copy in early + late:
        copy.start()
    place[...] = jnp.zeros_like(place)
    flat[...] = jnp.zeros_like(flat)

    for copy in early:
        copy.wait()
    for m in range(MB):
        place[m, 0:2, 0:TOK] = index_in[m].astype(F32)
        place[m, 2:4, 0:TOK] = scores_in[m]
    placed = pltpu.roll(place[0], c * ROWS, 1) + pltpu.roll(place[1], c * ROWS + TOK, 1)
    ids_in[e] = placed[0:2]

    def square(k, total):
        block = own_acts[:, span(k, SLICE)].astype(F32)
        return total + block * block

    squares = lax.fori_loop(0, GROUP, square, jnp.zeros((ROWS, SLICE), F32))
    inverse = lax.rsqrt(jnp.sum(squares, axis=1, keepdims=True) * (1.0 / WIDTH) + 1e-05)
    flat[span(c, ROWS), :] = jnp.broadcast_to(inverse, (ROWS, LANES))
    inverse_row = jnp.transpose(flat[...])[0:1]
    first = inverse_row / (1.0 + jnp.exp(placed[3:4] - placed[2:3]))
    second = inverse_row / (1.0 + jnp.exp(placed[2:3] - placed[3:4]))
    gates_in[c] = jnp.concatenate([first, second], axis=0)
    pl.semaphore_wait(barrier, GROUP)

    def remote(src, dst, ss, rs, section, device):
        return pltpu.make_async_remote_copy(
            src_ref=src,
            dst_ref=dst,
            send_sem=ss,
            recv_sem=rs,
            device_id=(section, device),
            device_id_type=MESH,
        )

    def acts_copy(device, slot):
        src = acts.at[:, span(device, SLICE)]
        return remote(src, acts_in.at[slot], acts_ss.at[device], acts_rs.at[slot], s, device)

    def down_copy(device, slot):
        src = down.at[:, span(device, SLICE)]
        return remote(src, down_in.at[slot], down_ss.at[device], down_rs.at[slot], s, device)

    def up_copy(g):
        def copy(device, slot):
            src = up.at[:, piece(device, g)]
            return remote(src, up_in.at[g, slot], up_ss.at[g, device], up_rs.at[g, slot], s, device)

        return copy

    def ids_copy(device, slot):
        return remote(ids_in.at[slot], ids_in.at[slot], ids_ss.at[device], ids_rs.at[slot], s, device)

    def gates_copy(slot):
        return remote(
            gates_in.at[slot], gates_in.at[slot], gates_ss, gates_rs, s, sibling
        )

    def part_copy(device, slot):
        src = part.at[lax.rem(device, 2), :, span(device // 2, BLOCK)]
        return remote(src, red.at[slot], part_ss.at[device], part_rs.at[slot], s, device)

    def low_copy(device, slot):
        return remote(low.at[slot], low.at[slot], low_ss.at[device], low_rs.at[slot], s, device)

    def out_copy(g):
        def copy(device, slot):
            return remote(
                send_out.at[g, device], hand.at[g, slot], out_ss.at[g, device], out_rs.at[g, slot], s, device
            )

        return copy

    def hand_copy(g, slot, own):
        src = send_out if own else hand
        return remote(
            src.at[g, slot],
            out.at[:, piece(slot, g)],
            hand_ss.at[g, slot],
            hand_rs.at[g, slot],
            s_next,
            e,
        )

    def next_copy(k):
        src, dst = (
            (acts_in.at[:, :, pl.ds(0, LANES)], acts_prev),
            (ids_in, ids_prev),
            (up_in.at[0], up_prev),
            (low, low_prev),
        )[k]
        return remote(src, dst, next_ss.at[k], next_rs.at[k], s_next, e)

    def last_copy(device, slot):
        return remote(
            send_out.at[0, device], out.at[:, piece(slot, 0)], out_ss.at[0, device], out_rs.at[0, slot], s, device
        )

    def send(copy):
        peers(lambda device: copy(device, e).start())

    def sent(copy):
        peers(lambda device: copy(device, e).wait_send())

    def received(copy):
        peers(lambda device: copy(device, device).wait_recv())

    gates_copy(c).start()
    send(ids_copy)
    send(down_copy)
    for device in others:
        down_copy(device, e).wait_send()
        acts_copy(device, e).start()
    for copy in late:
        copy.wait()
    received(ids_copy)
    next_copy(1).start()
    received(down_copy)

    def pick_block(q):
        tokens = acts_in[span(q, 2)].reshape(BLOCK, SLICE).astype(F32)
        scaled = (tokens * gain_in[...]).astype(BF16)
        both = ids_in[2 * q] + ids_in[2 * q + 1]
        picked = [jnp.zeros((RANK, BLOCK), F32) for _ in range(2)]
        for m in range(4):
            block = down_in[4 * m : 4 * m + 4].reshape(256, SLICE)
            product = lax.dot_general(block, scaled, (((1,), (1,)), ((), ())), preferred_element_type=F32)
            for g in range(16):
                rows = product[g * RANK : (g + 1) * RANK]
                for k in range(2):
                    picked[k] = jnp.where(both[k : k + 1] == float(m * 16 + g), rows, picked[k])
        for k in range(2):
            part[k, :, span(q, BLOCK)] = picked[k].astype(part.dtype)

    def pick_step(j):
        hops = 4 + ((j + 1) // 2) * (1 - 2 * lax.rem(j, 2))
        q = lax.rem(z + CHIPS - hops, CHIPS)
        for device in (2 * q + 1 - c, 2 * q + c):
            acts_copy(device, device).wait_recv()
        pick_block(q)
        for device in (2 * q + 1 - c, 2 * q + c):
            part_copy(device, e).start()
            up_copy(0)(device, e).start()

    each(CHIPS - 1, pick_step)
    acts_copy(sibling, sibling).wait_recv()
    next_copy(0).start()
    pick_block(z)
    part_copy(sibling, e).start()
    up_copy(0)(sibling, e).start()
    red[e] = part[c, :, span(z, BLOCK)]
    N1 = 11
    for device in others[:N1]:
        up_copy(1)(device, e).start()
    received(up_copy(0))
    next_copy(2).start()
    received(part_copy)
    gates_copy(1 - c).wait_recv()

    total = red[0].astype(F32)
    for k in range(1, GROUP):
        total = total + red[k].astype(F32)
    gates = gates_in[0] + gates_in[1]
    low[e] = (total * jnp.where(c == 0, gates[0:1], gates[1:2])).astype(BF16)
    send(low_copy)
    for device in others[N1:]:
        up_copy(1)(device, e).start()
    send(up_copy(2))
    received(low_copy)
    next_copy(3).start()


    def mix(ids, lows_in, result):
        def mix_step(q):
            both = ids[2 * q] + ids[2 * q + 1]
            lows = [lows_in[2 * q].astype(F32), lows_in[2 * q + 1].astype(F32)]
            for g in range(8):
                pieces = []
                for h in range(8):
                    expert = float(g * 8 + h)
                    rows = jnp.where(both[1:2] == expert, lows[1], 0.0)
                    pieces.append(jnp.where(both[0:1] == expert, lows[0], rows))
                tile = jnp.concatenate(pieces, axis=0)
                result[q, :, g * LANES : (g + 1) * LANES] = jnp.transpose(tile).astype(BF16)

        each(CHIPS, mix_step)

    def out_part(g, weights_in, table, base_in, start):
        weights = weights_in[...].reshape(EXPERTS * RANK, LANES)
        for pair in PAIRS:
            chips = [lax.rem(z + hops, CHIPS) for hops in pair]
            rows = jnp.concatenate([table[q] for q in chips], axis=0)
            delta = jnp.dot(rows, weights, preferred_element_type=F32)
            for k, (hops, q) in enumerate(zip(pair, chips)):
                base = base_in(q).reshape(BLOCK, LANES).astype(F32)
                mine = delta[k * BLOCK : (k + 1) * BLOCK]
                send_out[g, span(q, 2)] = (base + mine).astype(BF16).reshape(2, ROWS, LANES)
                if hops == 0:
                    start(sibling)
                else:
                    start(2 * q + 1 - c)
                    start(2 * q + c)

    def own_part(g):
        received(up_copy(g))
        out_part(
            g,
            up_in.at[g],
            mixed,
            lambda q: acts_in[span(q, 2), :, g * LANES : (g + 1) * LANES],
            lambda device: out_copy(g)(device, e).start(),
        )
        hand_copy(g, e, True).start()

    arrivals = [sibling]
    for hops in NEAR[1:]:
        other = lax.rem(z + hops, CHIPS) * 2
        arrivals += [other + 1 - c, other + c]

    def forward(g, devices):
        for device in devices:
            out_copy(g)(device, device).wait_recv()
            hand_copy(g, device, False).start()

    mix(ids_in, low, mixed)
    own_part(1)
    own_part(2)
    F1 = 5
    forward(1, arrivals[:F1])
    for k in range(4):
        next_copy(k).wait_recv()
    mix(ids_prev, low_prev, mixed_prev)
    out_part(
        0,
        up_prev,
        mixed_prev,
        lambda q: acts_prev[span(q, 2)],
        lambda device: last_copy(device, e).start(),
    )
    last = pltpu.make_async_copy(send_out.at[0, e], out.at[:, piece(e, 0)], local_sem.at[9])
    last.start()
    forward(1, arrivals[F1:])
    forward(2, arrivals)

    for g in range(1, PARTS):
        sent(out_copy(g))
        peers(lambda device: hand_copy(g, device, False).wait())
        hand_copy(g, e, True).wait()
    received(last_copy)
    sent(last_copy)
    last.wait()
    for k in range(4):
        next_copy(k).wait_send()
    for g in range(PARTS):
        sent(up_copy(g))
    gates_copy(c).wait_send()
    sent(acts_copy)
    sent(ids_copy)
    sent(part_copy)
    sent(low_copy)


def local(acts, index, scores, gain, down, up):
    dma = pltpu.SemaphoreType.DMA
    space = pl.BlockSpec(memory_space=pl.ANY)
    return pl.pallas_call(
        kernel,
        out_shape=jax.ShapeDtypeStruct((ROWS, WIDTH), acts.dtype),
        in_specs=[pl.BlockSpec(memory_space=pltpu.HBM)] * 6,
        out_specs=space,
        scratch_shapes=[
            pltpu.VMEM((ROWS, WIDTH), BF16),
            pltpu.VMEM((GROUP, ROWS, SLICE), BF16),
            pltpu.VMEM((GROUP, ROWS, SLICE), BF16),
            pltpu.VMEM((PARTS, GROUP, ROWS, LANES), BF16),
            pltpu.VMEM((1, SLICE), F32),
            pltpu.VMEM((MB, 2, TOK), jnp.int32),
            pltpu.VMEM((MB, 2, TOK), F32),
            pltpu.VMEM((MB, 8, LANES), F32),
            pltpu.VMEM((LANES, LANES), F32),
            pltpu.VMEM((GROUP, 2, LANES), F32),
            pltpu.VMEM((2, 2, LANES), F32),
            pltpu.VMEM((2, RANK, GROUP * ROWS), BF16),
            pltpu.VMEM((GROUP, RANK, BLOCK), BF16),
            pltpu.VMEM((GROUP, RANK, BLOCK), BF16),
            pltpu.VMEM((CHIPS, BLOCK, EXPERTS * RANK), BF16),
            pltpu.VMEM((CHIPS, BLOCK, EXPERTS * RANK), BF16),
            pltpu.VMEM((GROUP, ROWS, LANES), BF16),
            pltpu.VMEM((GROUP, ROWS, LANES), BF16),
            pltpu.VMEM((GROUP, 2, LANES), F32),
            pltpu.VMEM((GROUP, RANK, BLOCK), BF16),
            pltpu.VMEM((PARTS, GROUP, ROWS, LANES), BF16),
            pltpu.VMEM((PARTS, GROUP, ROWS, LANES), BF16),
            dma((10,)),
        ]
        + [dma((GROUP,))] * 4
        + [dma((PARTS, GROUP))] * 2
        + [dma((GROUP,))] * 2
        + [dma] * 2
        + [dma((GROUP,))] * 4
        + [dma((PARTS, GROUP))] * 4
        + [dma((4,))] * 2,
        compiler_params=pltpu.CompilerParams(
            collective_id=0, has_side_effects=True, vmem_limit_bytes=60 << 20
        ),
        cost_estimate=pl.CostEstimate(
            flops=4 * 1024 * 1024 * SLICE, bytes_accessed=4 * 786432, transcendentals=0
        ),
        name="relay",
    )(
        acts.reshape(ROWS, WIDTH),
        jnp.swapaxes(index, 2, 3),
        jnp.swapaxes(scores, 2, 3),
        gain,
        down.reshape(ROWS, WIDTH),
        up.reshape(ROWS, WIDTH),
    ).reshape(acts.shape)


def solution(mesh):
    return jax.shard_map(
        local,
        mesh=mesh,
        in_specs=(
            P("section", None, "expert", None),
            P("section", None, "expert", None),
            P("section", None, "expert", None),
            P("section", None),
            P("section", "expert", None, None),
            P("section", "expert", None, None),
        ),
        out_specs=P("section", None, "expert", None),
        check_vma=False,
    )
```

```python
import jax
import jax.numpy as jnp
from jax import lax
from jax.experimental import pallas as pl
from jax.experimental.pallas import tpu as pltpu
from jax.sharding import PartitionSpec as P

MESH = pl.DeviceIdType.MESH
SECTIONS = 32
CHIPS = 8
GROUP = 16
MB = 2
TOK = 32
ROWS = MB * TOK
RANK = 16
LOCAL_EXPERTS = 4
EXPERTS = GROUP * LOCAL_EXPERTS
WIDTH = 6144
SLICE = WIDTH // GROUP
LANES = 128
PARTS = SLICE // LANES
BLOCK = 2 * ROWS
ORDER = (
    (0, 1), (4, 1), (4, 0), (3, 1), (3, 0), (5, 1), (5, 0), (2, 1),
    (2, 0), (6, 1), (6, 0), (1, 1), (1, 0), (7, 1), (7, 0),
)
NEAR = (0, 1, 7, 2, 6, 3, 5, 4)
PAIRS = ((0, 1), (7, 2), (6, 3), (5, 4))
F32 = jnp.float32
BF16 = jnp.bfloat16


def kernel(
    acts,
    index,
    scores,
    gain,
    down,
    up,
    out,
    own_acts,
    acts_in,
    down_in,
    up_in,
    gain_in,
    index_in,
    scores_in,
    place,
    flat,
    ids_in,
    gates_in,
    part,
    red,
    low,
    mixed,
    mixed_prev,
    acts_prev,
    up_prev,
    ids_prev,
    low_prev,
    send_out,
    hand,
    local_sem,
    acts_ss,
    acts_rs,
    down_ss,
    down_rs,
    up_ss,
    up_rs,
    ids_ss,
    ids_rs,
    gates_ss,
    gates_rs,
    part_ss,
    part_rs,
    low_ss,
    low_rs,
    out_ss,
    out_rs,
    hand_ss,
    hand_rs,
    next_ss,
    next_rs,
    pass_ss,
    pass_rs,
):
    s = lax.axis_index("section")
    e = lax.axis_index("expert")
    z = e // 2
    c = lax.rem(e, 2)
    sibling = 2 * z + 1 - c
    s_next = lax.rem(s + 1, SECTIONS)
    s_prev = lax.rem(s + SECTIONS - 1, SECTIONS)

    others = [lax.rem(z + hops, CHIPS) * 2 + lax.rem(c + flip, 2) for hops, flip in ORDER]

    def span(k, width):
        return pl.ds(pl.multiple_of(k * width, width), width)

    def piece(device, g):
        return pl.ds(pl.multiple_of(device * SLICE + g * LANES, LANES), LANES)

    def each(count, body):
        def step(i, carry):
            body(i)
            return carry

        lax.fori_loop(0, count, step, 0)

    def peers(body):
        for device in others:
            body(device)

    barrier = pltpu.get_barrier_semaphore()

    def greet(device):
        pl.semaphore_signal(barrier, inc=1, device_id=(s, device), device_id_type=MESH)

    peers(greet)
    pl.semaphore_signal(barrier, inc=1, device_id=(s_prev, e), device_id_type=MESH)

    early = [
        pltpu.make_async_copy(acts, own_acts, local_sem.at[0]),
        pltpu.make_async_copy(index.at[0], index_in, local_sem.at[1]),
        pltpu.make_async_copy(scores.at[0], scores_in, local_sem.at[2]),
    ]
    late = [
        pltpu.make_async_copy(gain.at[:, span(e, SLICE)], gain_in, local_sem.at[3]),
        pltpu.make_async_copy(acts.at[:, span(e, SLICE)], acts_in.at[e], local_sem.at[4]),
        pltpu.make_async_copy(down.at[:, span(e, SLICE)], down_in.at[e], local_sem.at[5]),
    ]
    for g in range(PARTS):
        late.append(pltpu.make_async_copy(up.at[:, piece(e, g)], up_in.at[g, e], local_sem.at[6 + g]))
    for copy in early + late:
        copy.start()
    place[...] = jnp.zeros_like(place)
    flat[...] = jnp.zeros_like(flat)

    for copy in early:
        copy.wait()
    for m in range(MB):
        place[m, 0:2, 0:TOK] = index_in[m].astype(F32)
        place[m, 2:4, 0:TOK] = scores_in[m]
    placed = pltpu.roll(place[0], c * ROWS, 1) + pltpu.roll(place[1], c * ROWS + TOK, 1)
    ids_in[e] = placed[0:2]

    def square(k, total):
        block = own_acts[:, span(k, SLICE)].astype(F32)
        return total + block * block

    squares = lax.fori_loop(0, GROUP, square, jnp.zeros((ROWS, SLICE), F32))
    inverse = lax.rsqrt(jnp.sum(squares, axis=1, keepdims=True) * (1.0 / WIDTH) + 1e-05)
    flat[span(c, ROWS), :] = jnp.broadcast_to(inverse, (ROWS, LANES))
    inverse_row = jnp.transpose(flat[...])[0:1]
    first = inverse_row / (1.0 + jnp.exp(placed[3:4] - placed[2:3]))
    second = inverse_row / (1.0 + jnp.exp(placed[2:3] - placed[3:4]))
    gates_in[c] = jnp.concatenate([first, second], axis=0)
    pl.semaphore_wait(barrier, GROUP)

    def remote(src, dst, ss, rs, section, device):
        return pltpu.make_async_remote_copy(
            src_ref=src,
            dst_ref=dst,
            send_sem=ss,
            recv_sem=rs,
            device_id=(section, device),
            device_id_type=MESH,
        )

    def acts_copy(device, slot):
        src = acts.at[:, span(device, SLICE)]
        return remote(src, acts_in.at[slot], acts_ss.at[device], acts_rs.at[slot], s, device)

    def down_copy(device, slot):
        src = down.at[:, span(device, SLICE)]
        return remote(src, down_in.at[slot], down_ss.at[device], down_rs.at[slot], s, device)

    def up_copy(g):
        def copy(device, slot):
            src = up.at[:, piece(device, g)]
            return remote(src, up_in.at[g, slot], up_ss.at[g, device], up_rs.at[g, slot], s, device)

        return copy

    def ids_copy(device, slot):
        return remote(ids_in.at[slot], ids_in.at[slot], ids_ss.at[device], ids_rs.at[slot], s, device)

    def gates_copy(slot):
        return remote(
            gates_in.at[slot], gates_in.at[slot], gates_ss, gates_rs, s, sibling
        )

    def part_copy(device, slot):
        src = part.at[lax.rem(device, 2), :, span(device // 2, BLOCK)]
        return remote(src, red.at[slot], part_ss.at[device], part_rs.at[slot], s, device)

    def low_copy(device, slot):
        return remote(low.at[slot], low.at[slot], low_ss.at[device], low_rs.at[slot], s, device)

    def pass_copy(slot):
        return remote(low.at[slot], low.at[slot], pass_ss.at[slot], pass_rs.at[slot], s, sibling)

    def out_copy(g):
        def copy(device, slot):
            return remote(
                send_out.at[g, device], hand.at[g, slot], out_ss.at[g, device], out_rs.at[g, slot], s, device
            )

        return copy

    def hand_copy(g, slot, own):
        src = send_out if own else hand
        return remote(
            src.at[g, slot],
            out.at[:, piece(slot, g)],
            hand_ss.at[g, slot],
            hand_rs.at[g, slot],
            s_next,
            e,
        )

    def next_copy(k):
        src, dst = (
            (acts_in.at[:, :, pl.ds(0, LANES)], acts_prev),
            (ids_in, ids_prev),
            (up_in.at[0], up_prev),
            (low, low_prev),
        )[k]
        return remote(src, dst, next_ss.at[k], next_rs.at[k], s_next, e)

    def last_copy(device, slot):
        return remote(
            send_out.at[0, device], out.at[:, piece(slot, 0)], out_ss.at[0, device], out_rs.at[0, slot], s, device
        )

    def send(copy):
        peers(lambda device: copy(device, e).start())

    def sent(copy):
        peers(lambda device: copy(device, e).wait_send())

    def received(copy):
        peers(lambda device: copy(device, device).wait_recv())

    gates_copy(c).start()
    send(ids_copy)
    send(down_copy)
    for device in others:
        down_copy(device, e).wait_send()
        acts_copy(device, e).start()
    for copy in late:
        copy.wait()
    received(ids_copy)
    next_copy(1).start()
    received(down_copy)

    def pick_block(q):
        tokens = acts_in[span(q, 2)].reshape(BLOCK, SLICE).astype(F32)
        scaled = (tokens * gain_in[...]).astype(BF16)
        both = ids_in[2 * q] + ids_in[2 * q + 1]
        picked = [jnp.zeros((RANK, BLOCK), F32) for _ in range(2)]
        for m in range(4):
            block = down_in[4 * m : 4 * m + 4].reshape(256, SLICE)
            product = lax.dot_general(block, scaled, (((1,), (1,)), ((), ())), preferred_element_type=F32)
            for g in range(16):
                rows = product[g * RANK : (g + 1) * RANK]
                for k in range(2):
                    picked[k] = jnp.where(both[k : k + 1] == float(m * 16 + g), rows, picked[k])
        for k in range(2):
            part[k, :, span(q, BLOCK)] = picked[k].astype(part.dtype)

    def pick_step(j):
        hops = 4 + ((j + 1) // 2) * (1 - 2 * lax.rem(j, 2))
        q = lax.rem(z + CHIPS - hops, CHIPS)
        for device in (2 * q + 1 - c, 2 * q + c):
            acts_copy(device, device).wait_recv()
        pick_block(q)
        for device in (2 * q + 1 - c, 2 * q + c):
            part_copy(device, e).start()
            up_copy(0)(device, e).start()

    acts_copy(sibling, sibling).wait_recv()
    pick_block(z)
    part_copy(sibling, e).start()
    up_copy(0)(sibling, e).start()
    red[e] = part[c, :, span(z, BLOCK)]
    each(CHIPS - 1, pick_step)
    next_copy(0).start()
    N1 = 15
    for device in others[:N1]:
        up_copy(1)(device, e).start()
    received(part_copy)
    gates_copy(1 - c).wait_recv()

    total = red[0].astype(F32)
    for k in range(1, GROUP):
        total = total + red[k].astype(F32)
    gates = gates_in[0] + gates_in[1]
    low[e] = (total * jnp.where(c == 0, gates[0:1], gates[1:2])).astype(BF16)
    low_peers = [lax.rem(z + hops, CHIPS) * 2 + c for hops in (4, 3, 5, 2, 6, 1, 7)]
    for device in low_peers + [sibling]:
        low_copy(device, e).start()
    for device in others[N1:]:
        up_copy(1)(device, e).start()
    send(up_copy(2))
    received(up_copy(0))
    next_copy(2).start()
    def mix(ids, lows_in, result):
        def mix_step(q):
            both = ids[2 * q] + ids[2 * q + 1]
            lows = [lows_in[2 * q].astype(F32), lows_in[2 * q + 1].astype(F32)]
            for g in range(8):
                pieces = []
                for h in range(8):
                    expert = float(g * 8 + h)
                    rows = jnp.where(both[1:2] == expert, lows[1], 0.0)
                    pieces.append(jnp.where(both[0:1] == expert, lows[0], rows))
                tile = jnp.concatenate(pieces, axis=0)
                result[q, :, g * LANES : (g + 1) * LANES] = jnp.transpose(tile).astype(BF16)

        return mix_step

    def out_part(g, weights_in, table, base_in, start, prepare):
        weights = weights_in[...].reshape(EXPERTS * RANK, LANES)
        for pair in PAIRS:
            chips = [lax.rem(z + hops, CHIPS) for hops in pair]
            prepare(pair, chips)
            rows = jnp.concatenate([table[q] for q in chips], axis=0)
            delta = jnp.dot(rows, weights, preferred_element_type=F32)
            for k, (hops, q) in enumerate(zip(pair, chips)):
                base = base_in(q).reshape(BLOCK, LANES).astype(F32)
                mine = delta[k * BLOCK : (k + 1) * BLOCK]
                send_out[g, span(q, 2)] = (base + mine).astype(BF16).reshape(2, ROWS, LANES)
                if hops == 0:
                    start(sibling)
                else:
                    start(2 * q + 1 - c)
                    start(2 * q + c)

    def own_part(g, prepare):
        received(up_copy(g))
        out_part(
            g,
            up_in.at[g],
            mixed,
            lambda q: acts_in[span(q, 2), :, g * LANES : (g + 1) * LANES],
            lambda device: out_copy(g)(device, e).start(),
            prepare,
        )
        hand_copy(g, e, True).start()

    arrivals = [sibling]
    for hops in NEAR[1:]:
        other = lax.rem(z + hops, CHIPS) * 2
        arrivals += [other + 1 - c, other + c]

    def forward(g, devices):
        for device in devices:
            out_copy(g)(device, device).wait_recv()
            hand_copy(g, device, False).start()

    mix_own = mix(ids_in, low, mixed)
    mix_prev = mix(ids_prev, low_prev, mixed_prev)

    def mix_pair(mix_step, pair):
        each(2, lambda k: mix_step(lax.rem(z + pair[0] + k * (pair[1] - pair[0]), CHIPS)))

    def low_pair(pair, chips):
        for hops, q in zip(pair, chips):
            if hops:
                pass_copy(2 * q + 1 - c).wait_recv()
            else:
                low_copy(sibling, sibling).wait_recv()
        mix_pair(mix_own, pair)

    def nothing(pair, chips):
        pass

    for device in low_peers[::-1]:
        low_copy(device, device).wait_recv()
        pass_copy(device).start()
    own_part(1, low_pair)
    next_copy(3).start()
    own_part(2, nothing)
    F1 = 5
    forward(1, arrivals[:F1])
    for k in range(4):
        next_copy(k).wait_recv()
    out_part(
        0,
        up_prev,
        mixed_prev,
        lambda q: acts_prev[span(q, 2)],
        lambda device: last_copy(device, e).start(),
        lambda pair, chips: mix_pair(mix_prev, pair),
    )
    last = pltpu.make_async_copy(send_out.at[0, e], out.at[:, piece(e, 0)], local_sem.at[9])
    last.start()
    forward(1, arrivals[F1:])
    forward(2, arrivals)

    for g in range(1, PARTS):
        sent(out_copy(g))
        peers(lambda device: hand_copy(g, device, False).wait())
        hand_copy(g, e, True).wait()
    received(last_copy)
    sent(last_copy)
    last.wait()
    for k in range(4):
        next_copy(k).wait_send()
    for g in range(PARTS):
        sent(up_copy(g))
    gates_copy(c).wait_send()
    sent(acts_copy)
    sent(ids_copy)
    sent(part_copy)
    for device in low_peers:
        low_copy(device, e).wait_send()
        pass_copy(device).wait_send()
    low_copy(sibling, e).wait_send()


def local(acts, index, scores, gain, down, up):
    dma = pltpu.SemaphoreType.DMA
    space = pl.BlockSpec(memory_space=pl.ANY)
    return pl.pallas_call(
        kernel,
        out_shape=jax.ShapeDtypeStruct((ROWS, WIDTH), acts.dtype),
        in_specs=[pl.BlockSpec(memory_space=pltpu.HBM)] * 6,
        out_specs=space,
        scratch_shapes=[
            pltpu.VMEM((ROWS, WIDTH), BF16),
            pltpu.VMEM((GROUP, ROWS, SLICE), BF16),
            pltpu.VMEM((GROUP, ROWS, SLICE), BF16),
            pltpu.VMEM((PARTS, GROUP, ROWS, LANES), BF16),
            pltpu.VMEM((1, SLICE), F32),
            pltpu.VMEM((MB, 2, TOK), jnp.int32),
            pltpu.VMEM((MB, 2, TOK), F32),
            pltpu.VMEM((MB, 8, LANES), F32),
            pltpu.VMEM((LANES, LANES), F32),
            pltpu.VMEM((GROUP, 2, LANES), F32),
            pltpu.VMEM((2, 2, LANES), F32),
            pltpu.VMEM((2, RANK, GROUP * ROWS), BF16),
            pltpu.VMEM((GROUP, RANK, BLOCK), BF16),
            pltpu.VMEM((GROUP, RANK, BLOCK), BF16),
            pltpu.VMEM((CHIPS, BLOCK, EXPERTS * RANK), BF16),
            pltpu.VMEM((CHIPS, BLOCK, EXPERTS * RANK), BF16),
            pltpu.VMEM((GROUP, ROWS, LANES), BF16),
            pltpu.VMEM((GROUP, ROWS, LANES), BF16),
            pltpu.VMEM((GROUP, 2, LANES), F32),
            pltpu.VMEM((GROUP, RANK, BLOCK), BF16),
            pltpu.VMEM((PARTS, GROUP, ROWS, LANES), BF16),
            pltpu.VMEM((PARTS, GROUP, ROWS, LANES), BF16),
            dma((10,)),
        ]
        + [dma((GROUP,))] * 4
        + [dma((PARTS, GROUP))] * 2
        + [dma((GROUP,))] * 2
        + [dma] * 2
        + [dma((GROUP,))] * 4
        + [dma((PARTS, GROUP))] * 4
        + [dma((4,))] * 2
        + [dma((GROUP,))] * 2,
        compiler_params=pltpu.CompilerParams(
            collective_id=0, has_side_effects=True, vmem_limit_bytes=60 << 20
        ),
        cost_estimate=pl.CostEstimate(
            flops=4 * 1024 * 1024 * SLICE, bytes_accessed=4 * 786432, transcendentals=0
        ),
        name="relay",
    )(
        acts.reshape(ROWS, WIDTH),
        jnp.swapaxes(index, 2, 3),
        jnp.swapaxes(scores, 2, 3),
        gain,
        down.reshape(ROWS, WIDTH),
        up.reshape(ROWS, WIDTH),
    ).reshape(acts.shape)


def solution(mesh):
    return jax.shard_map(
        local,
        mesh=mesh,
        in_specs=(
            P("section", None, "expert", None),
            P("section", None, "expert", None),
            P("section", None, "expert", None),
            P("section", None),
            P("section", "expert", None, None),
            P("section", "expert", None, None),
        ),
        out_specs=P("section", None, "expert", None),
        check_vma=False,
    )
```
